512 devices in a mesh: row: 16 (over x_hi, z), col: 32 (over x_lo, y, core).
Axes of the slice: x: 4 (x_hi: 2, x_lo: 2; x = x_hi * 2 + x_lo), y: 8, z: 8, core: 2. Of those that a mesh axis runs over, the one named last changes fastest.
Arguments:
- tokens: bfloat16 [512, 12288], P('col', 'row'), may hold values from -6 to 6
- expand: bfloat16 [12288, 24576], P('row', 'col'), may hold values from -0.0546875 to 0.0546875
- project: bfloat16 [24576, 12288], P('col', 'row'), may hold values from -0.0390625 to 0.0390625
- out_grad: bfloat16 [512, 12288], P('col', 'row'), may hold values from -6 to 6
Outputs:
- layer_out: bfloat16 [512, 12288], P('col', 'row')
- token_grad: bfloat16 [512, 12288], P('col', 'row')
- expand_grad: bfloat16 [12288, 24576], P('row', 'col')
- project_grad: bfloat16 [24576, 12288], P('col', 'row')
The draws below stay inside these ranges and needn't reach their ends.
All inputs are finite; a program needn't handle non-finite values.
Results may differ from the reference program's by a relative error of at most 0.0049.
Values may be sent and summed in bfloat16 or wider, within the bound.
No kernel may reach another device: no remote copies, remote signals or barrier semaphores. Data moves between devices by JAX's collectives and lax.ppermute only.
A program may use at most 64 MiB of HBM per device.

```python
import math
import jax
import jax.numpy as jnp
from jax import lax

D = 12288
FF = 24576
TOKENS = 512


def shard_levels(own_key, dims, split, smallest, top_value):
    gain, own = 1.0, jax.random.fold_in(own_key, 6)
    for axis_at, blocks in split:
        steps = jnp.exp(jax.random.uniform(jax.random.fold_in(own, axis_at), (blocks,), jnp.float32, smallest / len(split), top_value / len(split)))
        gain = gain * jnp.repeat(steps, dims[axis_at] // blocks).reshape([-1 if axis == axis_at else 1 for axis in range(len(dims))])
    return gain


def normal_values(stream_key, shape, scale, limit, cuts=(), dtype=jnp.bfloat16):
    values = scale * jax.random.normal(stream_key, shape, jnp.float32)
    if cuts:
        values = values * shard_levels(stream_key, shape, cuts, -0.22, 0.18)
    return jnp.clip(values, -limit, limit).astype(dtype)


def setup_inputs(seed: int = 0) -> dict:
    splits = jax.random.split(jax.random.key(seed), 5)
    return {
        "tokens": normal_values(splits[0], (TOKENS, D), 1.0, 6.0, ((0, 32), (1, 16))),
        "expand": normal_values(splits[1], (D, FF), D ** -0.5, 0.0546875, ((0, 16), (1, 32))),
        "project": normal_values(splits[2], (FF, D), FF ** -0.5, 0.0390625, ((0, 32), (1, 16))),
        "out_grad": normal_values(splits[3], (TOKENS, D), 1.0, 6.0, ((0, 32), (1, 16))),
    }


SLOPE_C = math.sqrt(2.0 / math.pi)
CUBIC = 0.044715

def gelu_tanh(value):
    inner = SLOPE_C * (value + CUBIC * value * value * value)
    return 0.5 * value * (1.0 + jnp.tanh(inner))

def gelu_slope(value):
    inner = SLOPE_C * (value + CUBIC * value * value * value)
    tanh_value = jnp.tanh(inner)
    return 0.5 * (1.0 + tanh_value) + 0.5 * value * (1.0 - tanh_value * tanh_value) * SLOPE_C * (1.0 + 3.0 * CUBIC * value * value)

def reference(tokens, expand, project, out_grad):
    pre_act = jnp.dot(tokens, expand, preferred_element_type=jnp.float32)
    activated = gelu_tanh(pre_act).astype(jnp.bfloat16)
    layer_out = jnp.dot(activated, project, preferred_element_type=jnp.float32).astype(jnp.bfloat16)
    back_total = lax.dot_general(out_grad, project, (((1,), (1,)), ((), ())), preferred_element_type=jnp.float32)
    pre_grad = (back_total * gelu_slope(pre_act)).astype(jnp.bfloat16)
    token_grad = lax.dot_general(pre_grad, expand, (((1,), (1,)), ((), ())), preferred_element_type=jnp.float32).astype(jnp.bfloat16)
    factor = 1.0 / math.sqrt(TOKENS)
    expand_grad = (lax.dot_general(tokens, pre_grad, (((0,), (0,)), ((), ())), preferred_element_type=jnp.float32) * factor).astype(jnp.bfloat16)
    project_grad = (lax.dot_general(activated, out_grad, (((0,), (0,)), ((), ())), preferred_element_type=jnp.float32) * factor).astype(jnp.bfloat16)
    return (layer_out, token_grad, expand_grad, project_grad)
```

```python
import math

import jax
import jax.numpy as jnp
from jax import lax
from jax.sharding import PartitionSpec as P

SLOPE_C = math.sqrt(2.0 / math.pi)
CUBIC = 0.044715
CORES = 2


def gelu_and_slope(value):
    inner = SLOPE_C * (value + CUBIC * value * value * value)
    tanh_value = jnp.tanh(inner)
    gelu = 0.5 * value * (1.0 + tanh_value)
    slope = 0.5 * (1.0 + tanh_value) + 0.5 * value * (1.0 - tanh_value * tanh_value) * SLOPE_C * (
        1.0 + 3.0 * CUBIC * value * value
    )
    return gelu, slope


def same_core_groups(cols):
    return [list(range(core, cols, CORES)) for core in range(CORES)]


def swap_cores(block):
    cols = lax.axis_size("col")
    return lax.ppermute(block, "col", [(at, at ^ 1) for at in range(cols)])


def spread(block, members, axis, groups):
    copies = jnp.broadcast_to(block[None], (members, *block.shape))
    return lax.all_to_all(copies, axis, 0, 0, axis_index_groups=groups)


def exchange(parts, axis, groups):
    return jnp.sum(
        lax.all_to_all(parts, axis, 0, 0, axis_index_groups=groups).astype(jnp.float32), axis=0
    )


def matmul(left, right, contract):
    return lax.dot_general(left, right, (contract, ((), ())), preferred_element_type=jnp.float32)


def shards(tokens, expand, project, out_grad):
    rows, cols = lax.axis_size("row"), lax.axis_size("col")
    chips = cols // CORES
    own = tokens.shape[0]
    hidden = expand.shape[1]
    features = tokens.shape[1]
    groups = same_core_groups(cols)
    factor = 1.0 / math.sqrt(own * cols)

    expand_two = jnp.concatenate([expand, swap_cores(expand)], axis=1)
    project_two = jnp.concatenate([project, swap_cores(project)], axis=0)
    panels = spread(jnp.concatenate([tokens, out_grad], axis=0), chips, "col", groups)
    half = chips * own
    tok_panel = panels[:, :own].reshape(half, features)
    cot_panel = panels[:, own:].reshape(half, features)
    tok_other, cot_other = swap_cores(tok_panel), swap_cores(cot_panel)

    pre_part = matmul(tok_panel, expand_two, ((1,), (0,))).astype(jnp.bfloat16)
    back_part = matmul(cot_panel, project_two, ((1,), (1,))).astype(jnp.bfloat16)
    share = half // rows
    sums = exchange(
        jnp.concatenate(
            [
                pre_part.reshape(rows, share, CORES * hidden),
                back_part.reshape(rows, share, CORES * hidden),
            ],
            axis=1,
        ),
        "row",
        None,
    )
    gelu, slope = gelu_and_slope(sums[:share])
    act = gelu.astype(jnp.bfloat16)
    grad = (sums[share:] * slope).astype(jnp.bfloat16)
    hiddens = spread(jnp.concatenate([act, grad], axis=0), rows, "row", None)
    act_panel = hiddens[:, :share].reshape(half, CORES * hidden)
    grad_panel = hiddens[:, share:].reshape(half, CORES * hidden)

    out_part = matmul(act_panel, project_two, ((1,), (0,))).astype(jnp.bfloat16)
    tok_part = matmul(grad_panel, expand_two, ((1,), (1,))).astype(jnp.bfloat16)
    outs = exchange(
        jnp.concatenate(
            [out_part.reshape(chips, own, features), tok_part.reshape(chips, own, features)], axis=1
        ),
        "col",
        groups,
    ).astype(jnp.bfloat16)

    act_other = swap_cores(act_panel[:, hidden:])
    grad_other = swap_cores(grad_panel[:, hidden:])
    project_grad = matmul(
        jnp.concatenate([act_panel[:, :hidden], act_other], axis=0),
        jnp.concatenate([cot_panel, cot_other], axis=0),
        ((0,), (0,)),
    )
    expand_grad = matmul(
        jnp.concatenate([tok_panel, tok_other], axis=0),
        jnp.concatenate([grad_panel[:, :hidden], grad_other], axis=0),
        ((0,), (0,)),
    )
    return (
        outs[:own],
        outs[own:],
        (expand_grad * factor).astype(jnp.bfloat16),
        (project_grad * factor).astype(jnp.bfloat16),
    )


def solution(mesh):
    placed = (P("col", "row"), P("row", "col"), P("col", "row"), P("col", "row"))
    return jax.shard_map(
        shards,
        mesh=mesh,
        in_specs=placed,
        out_specs=(P("col", "row"), P("col", "row"), P("row", "col"), P("col", "row")),
        check_vma=False,
    )
```

```python
import math

import jax
import jax.numpy as jnp
from jax import lax
from jax.sharding import PartitionSpec as P

SLOPE_C = math.sqrt(2.0 / math.pi)
CUBIC = 0.044715
CORES = 2
PAIR = 2


def gelu_and_slope(value):
    inner = SLOPE_C * (value + CUBIC * value * value * value)
    tanh_value = jnp.tanh(inner)
    gelu = 0.5 * value * (1.0 + tanh_value)
    slope = 0.5 * (1.0 + tanh_value) + 0.5 * value * (1.0 - tanh_value * tanh_value) * SLOPE_C * (
        1.0 + 3.0 * CUBIC * value * value
    )
    return gelu, slope


def col_groups(rows, cols):
    chips = cols // CORES
    groups = []
    for row in range(rows):
        mine = row // (rows // PAIR)
        for core in range(CORES):
            order = [half * (chips // PAIR) + at for half in (mine, 1 - mine) for at in range(chips // PAIR)]
            groups.append([row * cols + chip * CORES + core for chip in order])
    return groups


def half_row_groups(rows):
    size = rows // PAIR
    return [list(range(half * size, (half + 1) * size)) for half in range(PAIR)]


def swap_cores(block):
    cols = lax.axis_size("col")
    return lax.ppermute(block, "col", [(at, at ^ 1) for at in range(cols)])


def swap_halves(block):
    rows = lax.axis_size("row")
    return lax.ppermute(block, "row", [(at, (at + rows // PAIR) % rows) for at in range(rows)])


def exchange(parts, axis, groups):
    return lax.all_to_all(parts, axis, 0, 0, axis_index_groups=groups)


def added(parts):
    return jnp.sum(parts.astype(jnp.float32), axis=0)


def matmul(left, right, contract):
    return lax.dot_general(left, right, (contract, ((), ())), preferred_element_type=jnp.float32)


def shards(tokens, expand, project, out_grad):
    rows, cols = lax.axis_size("row"), lax.axis_size("col")
    chips, size = cols // CORES, rows // PAIR
    own, features = tokens.shape
    hidden = expand.shape[1]
    count = chips * own
    half = count // PAIR
    share = half // size
    over_col, over_z = col_groups(rows, cols), half_row_groups(rows)
    factor = 1.0 / math.sqrt(own * cols)
    both = ("row", "col")

    def copies(block, members):
        return jnp.broadcast_to(block[None], (members, *block.shape))

    def after(block, earlier):
        return lax.optimization_barrier((block, earlier))[0]

    tok = exchange(copies(tokens, chips), both, over_col)
    cot = exchange(after(copies(out_grad, chips), tok), both, over_col)
    tok, cot = tok.reshape(count, features), cot.reshape(count, features)
    expand_two = jnp.concatenate([expand, swap_cores(expand)], axis=1)
    project_two = jnp.concatenate([project, swap_cores(project)], axis=0)

    def row_parts(panel, weight, contract):
        theirs = swap_halves(matmul(panel[half:], weight, contract).astype(jnp.bfloat16))
        mine = matmul(panel[:half], weight, contract) + theirs.astype(jnp.float32)
        return mine.astype(jnp.bfloat16).reshape(size, share, CORES * hidden)

    pre_parts = row_parts(tok, expand_two, ((1,), (0,)))
    back_parts = row_parts(cot, project_two, ((1,), (1,)))
    pre_parts = exchange(after(pre_parts, cot), "row", over_z)
    gelu, slope = gelu_and_slope(added(pre_parts))
    act = copies(gelu.astype(jnp.bfloat16), size)
    mixed = exchange(jnp.concatenate([back_parts, act], axis=1), "row", over_z)
    grad = (added(mixed[:, :share]) * slope).astype(jnp.bfloat16)
    act_mine = mixed[:, share:].reshape(half, CORES * hidden)
    grad_mine = exchange(copies(grad, size), "row", over_z).reshape(half, CORES * hidden)
    act_panel = jnp.concatenate([act_mine, swap_halves(act_mine)], axis=0)
    grad_panel = jnp.concatenate([grad_mine, swap_halves(grad_mine)], axis=0)

    def col_parts(panel, weight, contract):
        parts = matmul(panel, weight, contract).astype(jnp.bfloat16)
        return parts.reshape(chips, own, features)

    out_parts = col_parts(act_panel, project_two, ((1,), (0,)))
    tok_parts = col_parts(grad_panel, expand_two, ((1,), (1,)))
    out_parts = exchange(after(out_parts, grad_mine), both, over_col)
    tok_parts = exchange(after(tok_parts, out_parts), both, over_col)
    layer_out = added(out_parts).astype(jnp.bfloat16)
    token_grad = added(tok_parts).astype(jnp.bfloat16)

    def all_tokens(panel):
        return jnp.concatenate([panel, swap_cores(panel)], axis=0)

    def hidden_tokens(panel):
        return jnp.concatenate([panel[:, :hidden], swap_cores(panel[:, hidden:])], axis=0)

    project_grad = matmul(hidden_tokens(act_panel), all_tokens(cot), ((0,), (0,)))
    expand_grad = matmul(all_tokens(tok), hidden_tokens(grad_panel), ((0,), (0,)))
    return (
        layer_out,
        token_grad,
        (expand_grad * factor).astype(jnp.bfloat16),
        (project_grad * factor).astype(jnp.bfloat16),
    )


def solution(mesh):
    placed = (P("col", "row"), P("row", "col"), P("col", "row"), P("col", "row"))
    return jax.shard_map(
        shards,
        mesh=mesh,
        in_specs=placed,
        out_specs=(P("col", "row"), P("col", "row"), P("row", "col"), P("col", "row")),
        check_vma=False,
    )
```

```python
import functools
import math

import jax
import jax.numpy as jnp
from jax import lax
from jax.experimental import pallas as pl
from jax.experimental.pallas import tpu as pltpu
from jax.sharding import PartitionSpec as P

SLOPE_C = math.sqrt(2.0 / math.pi)
CUBIC = 0.044715
CORES = 2
PAIR = 2
HIDE_FRONT = 1
HIDE_ACT = 1
HIDE_BACK = 100
F32, BF16 = jnp.float32, jnp.bfloat16
VMEM_BYTES = 12 << 20
IN_SMEM = pl.BlockSpec(memory_space=pltpu.SMEM)
IN_VMEM = pl.BlockSpec(memory_space=pltpu.VMEM)
ANYWHERE = pl.BlockSpec(memory_space=pl.ANY)


def gelu_and_slope(value):
    inner = SLOPE_C * (value + CUBIC * value * value * value)
    tanh_value = jnp.tanh(inner)
    gelu = 0.5 * value * (1.0 + tanh_value)
    slope = 0.5 * (1.0 + tanh_value) + 0.5 * value * (1.0 - tanh_value * tanh_value) * SLOPE_C * (
        1.0 + 3.0 * CUBIC * value * value
    )
    return gelu, slope


def col_groups(cols):
    return [list(range(core, cols, CORES)) for core in range(CORES)]


def swap_cores(block):
    cols = lax.axis_size("col")
    return lax.ppermute(block, "col", [(at, at ^ 1) for at in range(cols)])


def row_groups(rows):
    step = rows // PAIR
    return [list(range(at * step, (at + 1) * step)) for at in range(PAIR)]


def swap_halves(block):
    rows = lax.axis_size("row")
    return lax.ppermute(block, "row", [(at, (at + rows // PAIR) % rows) for at in range(rows)])


def exchange(parts, axis, groups):
    return lax.all_to_all(parts, axis, 0, 0, axis_index_groups=groups)


def after(block, earlier):
    return lax.optimization_barrier((block, earlier))[0]


def matmul(left, right, contract):
    return lax.dot_general(left, right, (contract, ((), ())), preferred_element_type=F32)


def times(left, right):
    return matmul(left, right, ((1,), (0,)))


def times_turned(left, right):
    return matmul(left, right, ((1,), (1,)))


def flat(block):
    return block.reshape(-1, block.shape[-1])


def array(*shape, dtype=BF16):
    return jax.ShapeDtypeStruct(shape, dtype)


def call(kernel, outs, flops, *args, ins=(), scratch=()):
    held = sum(math.prod(a.shape) * a.dtype.itemsize for a in (*args, *outs))
    one = len(outs) == 1
    return pl.pallas_call(
        kernel,
        out_shape=outs[0] if one else outs,
        in_specs=[
            ANYWHERE if at in ins else IN_SMEM if a.dtype == jnp.int32 else IN_VMEM for at, a in enumerate(args)
        ],
        out_specs=IN_VMEM if one else [IN_VMEM] * len(outs),
        scratch_shapes=scratch,
        compiler_params=pltpu.CompilerParams(vmem_limit_bytes=VMEM_BYTES),
        cost_estimate=pl.CostEstimate(flops=flops, bytes_accessed=held, transcendentals=0),
    )(*args)


def put_terms(out, dot, panel, near, far):
    hidden = out.shape[2] // CORES
    for side, weight in enumerate((near, far)):
        terms = dot(panel, weight[...]).astype(out.dtype)
        out[:, :, side * hidden : (side + 1) * hidden] = terms.reshape(*out.shape[:2], hidden)


def pre_kernel(panels, expand, expand_far, out, held, sem):
    load = pltpu.make_async_copy(panels.at[:, pl.ds(0, out.shape[1])], held, sem)
    load.start()
    load.wait()
    put_terms(out, times, flat(held[...]), expand, expand_far)


def back_kernel(other, which, panels, project, project_far, out, held, sem):
    size, own = out.shape[0], out.shape[1]
    half = 1 - which[0] if other else which[0]
    load = pltpu.make_async_copy(panels.at[pl.ds(half * size, size), pl.ds(own, own)], held, sem)
    load.start()
    load.wait()
    put_terms(out, times_turned, flat(held[...]), project, project_far)


def added(ref, stop):
    total = ref[0, :stop].astype(F32)
    for at in range(1, ref.shape[0]):
        total += ref[at, :stop].astype(F32)
    return total


def act_kernel(sums, act, slope):
    gelu, slope[...] = gelu_and_slope(added(sums, sums.shape[1]))
    act[...] = gelu.astype(BF16)


def merge_kernel(mine, came, act, mixed):
    share = act.shape[0]
    mixed[:, :share] = (mine[...] + came[...].astype(F32)).astype(BF16)
    block = act[...]
    for at in range(mixed.shape[0]):
        mixed[at, share:] = block


def grad_kernel(mixed, slope, act, out):
    share = slope.shape[0]
    act[...] = mixed[:, share:]
    grad = (added(mixed, share) * slope[...]).astype(BF16)
    for at in range(out.shape[0]):
        out[at] = grad


def out_kernel(which, act, act_far, project, project_far, out, keep, send):
    size, own, hidden = act.shape[0], out.shape[1], project.shape[0]
    for half, block in ((which[0], act[...]), (1 - which[0], act_far[...])):
        at = pl.ds(half * size, size)
        left, right = block[:, :, :hidden], block[:, :, hidden:]
        keep[at] = left
        send[at] = right
        terms = times(flat(left), project[...]) + times(flat(right), project_far[...])
        out[at] = terms.astype(BF16).reshape(size, own, out.shape[2])


def tok_kernel(grad, out_parts, expand, expand_far, out):
    own, hidden = out_parts.shape[1], expand.shape[1]
    block = flat(grad[...])
    terms = times_turned(block[:, :hidden], expand[...]) + times_turned(block[:, hidden:], expand_far[...])
    out[:, :own] = out_parts[...]
    out[:, own:] = terms.astype(BF16).reshape(out.shape[0], own, out.shape[2])


def pack_kernel(grad, keep, send):
    hidden = keep.shape[2]
    keep[...] = grad[:, :, :hidden]
    send[...] = grad[:, :, hidden:]


def weight_grads_kernel(factor, panels, panels_far, act, act_got, grad, grad_got, expand_grad, project_grad):
    own = panels.shape[1] // 2

    def sums(left, left_far, right, right_far):
        total = matmul(flat(left), flat(right), ((0,), (0,))) + matmul(flat(left_far), flat(right_far), ((0,), (0,)))
        return (total * factor).astype(BF16)

    project_grad[...] = sums(act[...], act_got[...], panels[:, own:], panels_far[:, own:])
    expand_grad[...] = sums(panels[:, :own], panels_far[:, :own], grad[...], grad_got[...])


def final_kernel(sums, layer_out, token_grad):
    own = layer_out.shape[0]
    total = added(sums, 2 * own).astype(BF16)
    layer_out[...] = total[:own]
    token_grad[...] = total[own:]


def shards(tokens, expand, project, out_grad):
    rows, cols = lax.axis_size("row"), lax.axis_size("col")
    chips = cols // CORES
    own, features = tokens.shape
    hidden = expand.shape[1]
    wide, share, size = CORES * hidden, chips * own // rows, rows // PAIR
    over_col, along_z = col_groups(cols), row_groups(rows)
    factor = 1.0 / math.sqrt(own * cols)
    work = 2 * chips * own * wide * features
    which = (lax.axis_index("row") // size).astype(jnp.int32).reshape(1)

    block = jnp.concatenate([tokens, out_grad], axis=0)
    copies = jnp.broadcast_to(block[None], (chips, *block.shape))
    project_far = swap_cores(after(project, copies))
    expand_far = swap_cores(after(expand, copies))
    panels = exchange(copies, "col", over_col)

    half_sums = array(size, share, wide)
    pre = call(
        pre_kernel,
        [array(rows, share, wide)],
        work,
        panels,
        expand,
        expand_far,
        ins=(0,),
        scratch=[pltpu.VMEM((chips, own, features), BF16), pltpu.SemaphoreType.DMA],
    )

    def back_terms(other, dtype, earlier):
        return call(
            functools.partial(back_kernel, other),
            [array(size, share, wide, dtype=dtype)],
            work // 2 * HIDE_FRONT,
            which,
            after(panels, earlier),
            project,
            project_far,
            ins=(1,),
            scratch=[pltpu.VMEM((size, own, features), BF16), pltpu.SemaphoreType.DMA],
        )

    theirs = back_terms(True, BF16, pre)
    came = swap_halves(theirs)
    mine = back_terms(False, F32, theirs)
    pre = exchange(pre, "row", None)
    act, slope = call(
        act_kernel, [array(share, wide), array(share, wide, dtype=F32)], work * HIDE_ACT, pre
    )
    mixed = call(merge_kernel, [array(size, 2 * share, wide)], 0, mine, came, act)
    mixed = exchange(mixed, "row", along_z)
    act, grad = call(grad_kernel, [half_sums, array(rows, share, wide)], 0, mixed, slope)
    act_far = swap_halves(act)
    grad = exchange(grad, "row", None)
    held = array(chips, own, hidden)
    out_parts, act, act_send = call(
        out_kernel,
        [array(chips, own, features), held, held],
        work * HIDE_BACK,
        which,
        act,
        act_far,
        project,
        project_far,
    )
    parts = call(
        tok_kernel, [array(chips, 2 * own, features)], work, grad, out_parts, expand, expand_far
    )
    sums = exchange(parts, "col", over_col)
    act_got = swap_cores(act_send)
    grad, grad_send = call(pack_kernel, [held, held], 0, after(grad, parts))
    grad_got = swap_cores(grad_send)
    panels_far = swap_cores(after(panels, parts))
    expand_grad, project_grad = call(
        functools.partial(weight_grads_kernel, factor),
        [array(features, hidden), array(hidden, features)],
        2 * work,
        panels,
        panels_far,
        act,
        act_got,
        grad,
        grad_got,
    )
    shard = array(own, features)
    layer_out, token_grad = call(final_kernel, [shard, shard], 0, after(sums, expand_grad))
    return (layer_out, token_grad, expand_grad, project_grad)


def solution(mesh):
    placed = (P("col", "row"), P("row", "col"), P("col", "row"), P("col", "row"))
    return jax.shard_map(
        shards,
        mesh=mesh,
        in_specs=placed,
        out_specs=(P("col", "row"), P("col", "row"), P("row", "col"), P("col", "row")),
        check_vma=False,
    )
```

```python
import functools
import math

import jax
import jax.numpy as jnp
from jax import lax
from jax.experimental import pallas as pl
from jax.experimental.pallas import tpu as pltpu
from jax.sharding import PartitionSpec as P

SLOPE_C = math.sqrt(2.0 / math.pi)
CUBIC = 0.044715
CORES = 2
PAIR = 2
HIDE_FRONT = 5
HIDE_ACT = 1
HIDE_PRE = 0
HIDE_TOK = 0
HIDE_SWAP = 1
HIDE_BACK = 100
F32, BF16 = jnp.float32, jnp.bfloat16
VMEM_BYTES = 12 << 20
IN_SMEM = pl.BlockSpec(memory_space=pltpu.SMEM)
IN_VMEM = pl.BlockSpec(memory_space=pltpu.VMEM)
ANYWHERE = pl.BlockSpec(memory_space=pl.ANY)


def gelu_and_slope(value):
    inner = SLOPE_C * (value + CUBIC * value * value * value)
    tanh_value = jnp.tanh(inner)
    gelu = 0.5 * value * (1.0 + tanh_value)
    slope = 0.5 * (1.0 + tanh_value) + 0.5 * value * (1.0 - tanh_value * tanh_value) * SLOPE_C * (
        1.0 + 3.0 * CUBIC * value * value
    )
    return gelu, slope


def col_groups(cols):
    return [list(range(core, cols, CORES)) for core in range(CORES)]


def swap_cores(block):
    cols = lax.axis_size("col")
    return lax.ppermute(block, "col", [(at, at ^ 1) for at in range(cols)])


def row_groups(rows):
    step = rows // PAIR
    return [list(range(at * step, (at + 1) * step)) for at in range(PAIR)]


def swap_halves(block):
    rows = lax.axis_size("row")
    return lax.ppermute(block, "row", [(at, (at + rows // PAIR) % rows) for at in range(rows)])


def exchange(parts, axis, groups):
    return lax.all_to_all(parts, axis, 0, 0, axis_index_groups=groups)


def after(block, earlier):
    return lax.optimization_barrier((block, earlier))[0]


def matmul(left, right, contract):
    return lax.dot_general(left, right, (contract, ((), ())), preferred_element_type=F32)


def times(left, right):
    return matmul(left, right, ((1,), (0,)))


def times_turned(left, right):
    return matmul(left, right, ((1,), (1,)))


def flat(block):
    return block.reshape(-1, block.shape[-1])


def array(*shape, dtype=BF16):
    return jax.ShapeDtypeStruct(shape, dtype)


def call(kernel, outs, flops, *args, ins=(), scratch=()):
    held = sum(math.prod(a.shape) * a.dtype.itemsize for a in (*args, *outs))
    one = len(outs) == 1
    return pl.pallas_call(
        kernel,
        out_shape=outs[0] if one else outs,
        in_specs=[
            ANYWHERE if at in ins else IN_SMEM if a.dtype == jnp.int32 else IN_VMEM for at, a in enumerate(args)
        ],
        out_specs=IN_VMEM if one else [IN_VMEM] * len(outs),
        scratch_shapes=scratch,
        compiler_params=pltpu.CompilerParams(vmem_limit_bytes=VMEM_BYTES),
        cost_estimate=pl.CostEstimate(flops=flops, bytes_accessed=held, transcendentals=0),
    )(*args)


def put_terms(out, dot, panel, near, far):
    hidden = out.shape[2] // CORES
    for side, weight in enumerate((near, far)):
        terms = dot(panel, weight[...]).astype(out.dtype)
        out[:, :, side * hidden : (side + 1) * hidden] = terms.reshape(*out.shape[:2], hidden)


def pre_kernel(panels, expand, expand_far, out, held, sem):
    load = pltpu.make_async_copy(panels.at[:, pl.ds(0, out.shape[1])], held, sem)
    load.start()
    load.wait()
    put_terms(out, times, flat(held[...]), expand, expand_far)


def back_kernel(other, which, panels, project, project_far, out, held, sem):
    size, own = out.shape[0], out.shape[1]
    half = 1 - which[0] if other else which[0]
    load = pltpu.make_async_copy(panels.at[pl.ds(half * size, size), pl.ds(own, own)], held, sem)
    load.start()
    load.wait()
    put_terms(out, times_turned, flat(held[...]), project, project_far)


def added(ref, stop):
    total = ref[0, :stop].astype(F32)
    for at in range(1, ref.shape[0]):
        total += ref[at, :stop].astype(F32)
    return total


def act_kernel(sums, act, slope):
    gelu, slope[...] = gelu_and_slope(added(sums, sums.shape[1]))
    act[...] = gelu.astype(BF16)


def merge_kernel(mine, came, act, mixed):
    share = act.shape[0]
    mixed[:, :share] = (mine[...] + came[...].astype(F32)).astype(BF16)
    block = act[...]
    for at in range(mixed.shape[0]):
        mixed[at, share:] = block


def grad_kernel(mixed, slope, act, out):
    share = slope.shape[0]
    act[...] = mixed[:, share:]
    grad = (added(mixed, share) * slope[...]).astype(BF16)
    for at in range(out.shape[0]):
        out[at] = grad


def out_kernel(which, act, act_far, project, project_far, out, keep, send):
    size, own, hidden = act.shape[0], out.shape[1], project.shape[0]
    for half, block in ((which[0], act[...]), (1 - which[0], act_far[...])):
        at = pl.ds(half * size, size)
        left, right = block[:, :, :hidden], block[:, :, hidden:]
        keep[at] = left
        send[at] = right
        terms = times(flat(left), project[...]) + times(flat(right), project_far[...])
        out[at] = terms.astype(BF16).reshape(size, own, out.shape[2])


def tok_kernel(grad, out_parts, expand, expand_far, out):
    own, hidden = out_parts.shape[1], expand.shape[1]
    block = flat(grad[...])
    terms = times_turned(block[:, :hidden], expand[...]) + times_turned(block[:, hidden:], expand_far[...])
    out[:, :own] = out_parts[...]
    out[:, own:] = terms.astype(BF16).reshape(out.shape[0], own, out.shape[2])


def pack_kernel(grad, keep, send):
    hidden = keep.shape[2]
    keep[...] = grad[:, :, :hidden]
    send[...] = grad[:, :, hidden:]


def weight_grads_kernel(factor, panels, panels_far, act, act_got, grad, grad_got, expand_grad, project_grad):
    own = panels.shape[1] // 2

    def sums(left, left_far, right, right_far):
        total = matmul(flat(left), flat(right), ((0,), (0,))) + matmul(flat(left_far), flat(right_far), ((0,), (0,)))
        return (total * factor).astype(BF16)

    project_grad[...] = sums(act[...], act_got[...], panels[:, own:], panels_far[:, own:])
    expand_grad[...] = sums(panels[:, :own], panels_far[:, :own], grad[...], grad_got[...])


def final_kernel(sums, layer_out, token_grad):
    own = layer_out.shape[0]
    total = added(sums, 2 * own).astype(BF16)
    layer_out[...] = total[:own]
    token_grad[...] = total[own:]


def shards(tokens, expand, project, out_grad):
    rows, cols = lax.axis_size("row"), lax.axis_size("col")
    chips = cols // CORES
    own, features = tokens.shape
    hidden = expand.shape[1]
    wide, share, size = CORES * hidden, chips * own // rows, rows // PAIR
    over_col, along_z = col_groups(cols), row_groups(rows)
    factor = 1.0 / math.sqrt(own * cols)
    work = 2 * chips * own * wide * features
    which = (lax.axis_index("row") // size).astype(jnp.int32).reshape(1)

    block = jnp.concatenate([tokens, out_grad], axis=0)
    copies = jnp.broadcast_to(block[None], (chips, *block.shape))
    project_far = swap_cores(after(project, copies))
    expand_far = swap_cores(after(expand, copies))
    panels = exchange(copies, "col", over_col)

    half_sums = array(size, share, wide)
    pre = call(
        pre_kernel,
        [array(rows, share, wide)],
        work * HIDE_PRE,
        panels,
        expand,
        expand_far,
        ins=(0,),
        scratch=[pltpu.VMEM((chips, own, features), BF16), pltpu.SemaphoreType.DMA],
    )

    def back_terms(other, dtype, earlier):
        return call(
            functools.partial(back_kernel, other),
            [array(size, share, wide, dtype=dtype)],
            work // 2 * HIDE_FRONT,
            which,
            after(panels, earlier),
            project,
            project_far,
            ins=(1,),
            scratch=[pltpu.VMEM((size, own, features), BF16), pltpu.SemaphoreType.DMA],
        )

    theirs = back_terms(True, BF16, pre)
    came = swap_halves(theirs)
    mine = back_terms(False, F32, theirs)
    pre = exchange(pre, "row", None)
    act, slope = call(
        act_kernel, [array(share, wide), array(share, wide, dtype=F32)], work * HIDE_ACT, pre
    )
    mixed = call(merge_kernel, [array(size, 2 * share, wide)], 0, mine, came, act)
    mixed = exchange(mixed, "row", along_z)
    act, grad = call(grad_kernel, [half_sums, array(rows, share, wide)], 0, mixed, slope)
    act_far = swap_halves(act)
    grad = exchange(grad, "row", None)
    held = array(chips, own, hidden)
    out_parts, act, act_send = call(
        out_kernel,
        [array(chips, own, features), held, held],
        work * HIDE_BACK,
        which,
        act,
        act_far,
        project,
        project_far,
    )
    parts = call(
        tok_kernel, [array(chips, 2 * own, features)], work * HIDE_TOK, grad, out_parts, expand, expand_far
    )
    sums = exchange(parts, "col", over_col)
    act_got = swap_cores(act_send)
    grad, grad_send = call(pack_kernel, [held, held], 0, after(grad, parts))
    grad_got = swap_cores(grad_send)
    panels_far = swap_cores(after(panels, parts))
    expand_grad, project_grad = call(
        functools.partial(weight_grads_kernel, factor),
        [array(features, hidden), array(hidden, features)],
        2 * work,
        panels,
        panels_far,
        act,
        act_got,
        grad,
        grad_got,
    )
    shard = array(own, features)
    layer_out, token_grad = call(final_kernel, [shard, shard], 0, after(sums, expand_grad))
    return (layer_out, token_grad, expand_grad, project_grad)


def solution(mesh):
    placed = (P("col", "row"), P("row", "col"), P("col", "row"), P("col", "row"))
    return jax.shard_map(
        shards,
        mesh=mesh,
        in_specs=placed,
        out_specs=(P("col", "row"), P("col", "row"), P("row", "col"), P("col", "row")),
        check_vma=False,
    )
```

```python
import functools
import math

import jax
import jax.numpy as jnp
from jax import lax
from jax.experimental import pallas as pl
from jax.experimental.pallas import tpu as pltpu
from jax.sharding import PartitionSpec as P

SLOPE_C = math.sqrt(2.0 / math.pi)
CUBIC = 0.044715
CORES = 2
PAIR = 2
UNIT = 600_000_000
COSTS = dict(pre=(100, 10), theirs=(2.5, 1), mine=(2.5, 1), act=(0, 1), merge=(0, 1), grad=(0, 1), out=(100, 1), layer=(1, 1), tok=(0, 1), pack=(2.5, 1), grads=(2, 1), final=(0, 1))
F32, BF16 = jnp.float32, jnp.bfloat16
VMEM_BYTES = 12 << 20
IN_SMEM = pl.BlockSpec(memory_space=pltpu.SMEM)
IN_VMEM = pl.BlockSpec(memory_space=pltpu.VMEM)
ANYWHERE = pl.BlockSpec(memory_space=pl.ANY)


def gelu_and_slope(value):
    inner = SLOPE_C * (value + CUBIC * value * value * value)
    tanh_value = jnp.tanh(inner)
    gelu = 0.5 * value * (1.0 + tanh_value)
    slope = 0.5 * (1.0 + tanh_value) + 0.5 * value * (1.0 - tanh_value * tanh_value) * SLOPE_C * (
        1.0 + 3.0 * CUBIC * value * value
    )
    return gelu, slope


def col_groups(cols):
    return [list(range(core, cols, CORES)) for core in range(CORES)]


def swap_cores(block):
    cols = lax.axis_size("col")
    return lax.ppermute(block, "col", [(at, at ^ 1) for at in range(cols)])


def row_groups(rows):
    step = rows // PAIR
    return [list(range(at * step, (at + 1) * step)) for at in range(PAIR)]


def swap_halves(block, axis):
    count = lax.axis_size(axis)
    return lax.ppermute(block, axis, [(at, (at + count // PAIR) % count) for at in range(count)])


def exchange(parts, axis, groups):
    return lax.all_to_all(parts, axis, 0, 0, axis_index_groups=groups)


def after(block, earlier):
    return lax.optimization_barrier((block, earlier))[0]


def matmul(left, right, contract):
    return lax.dot_general(left, right, (contract, ((), ())), preferred_element_type=F32)


def times(left, right):
    return matmul(left, right, ((1,), (0,)))


def times_turned(left, right):
    return matmul(left, right, ((1,), (1,)))


def flat(block):
    return block.reshape(-1, block.shape[-1])


def array(*shape, dtype=BF16):
    return jax.ShapeDtypeStruct(shape, dtype)


def call(kernel, name, outs, *args, ins=(), scratch=()):
    held = sum(math.prod(a.shape) * a.dtype.itemsize for a in (*args, *outs))
    one = len(outs) == 1
    products, touched = COSTS[name]
    return pl.pallas_call(
        kernel,
        out_shape=outs[0] if one else outs,
        in_specs=[
            ANYWHERE if at in ins else IN_SMEM if a.dtype == jnp.int32 else IN_VMEM for at, a in enumerate(args)
        ],
        out_specs=IN_VMEM if one else [IN_VMEM] * len(outs),
        scratch_shapes=scratch,
        compiler_params=pltpu.CompilerParams(vmem_limit_bytes=VMEM_BYTES),
        cost_estimate=pl.CostEstimate(
            flops=int(products * UNIT), bytes_accessed=int(touched * held), transcendentals=0
        ),
    )(*args)


def put_terms(out, dot, panel, near, far):
    hidden = out.shape[2] // CORES
    for side, weight in enumerate((near, far)):
        terms = dot(panel, weight[...]).astype(out.dtype)
        out[:, :, side * hidden : (side + 1) * hidden] = terms.reshape(*out.shape[:2], hidden)


def pre_kernel(panels, expand, expand_far, out, held, sem):
    load = pltpu.make_async_copy(panels.at[:, pl.ds(0, out.shape[1])], held, sem)
    load.start()
    load.wait()
    put_terms(out, times, flat(held[...]), expand, expand_far)


def back_kernel(other, which, panels, project, project_far, out, held, sem):
    size, own = out.shape[0], out.shape[1]
    half = 1 - which[0] if other else which[0]
    load = pltpu.make_async_copy(panels.at[pl.ds(half * size, size), pl.ds(own, own)], held, sem)
    load.start()
    load.wait()
    put_terms(out, times_turned, flat(held[...]), project, project_far)


def added(ref, stop):
    total = ref[0, :stop].astype(F32)
    for at in range(1, ref.shape[0]):
        total += ref[at, :stop].astype(F32)
    return total


def act_kernel(sums, act, slope):
    gelu, slope[...] = gelu_and_slope(added(sums, sums.shape[1]))
    act[...] = gelu.astype(BF16)


def merge_kernel(mine, came, act, mixed):
    share = act.shape[0]
    mixed[:, :share] = (mine[...] + came[...].astype(F32)).astype(BF16)
    block = act[...]
    for at in range(mixed.shape[0]):
        mixed[at, share:] = block


def grad_kernel(mixed, slope, act, out):
    share = slope.shape[0]
    act[...] = mixed[:, share:]
    grad = (added(mixed, share) * slope[...]).astype(BF16)
    for at in range(out.shape[0]):
        out[at] = grad


def out_kernel(which, act, act_far, project, project_far, stay, leave, keep, send):
    size, rows, hidden = act.shape[0], stay.shape[1], project.shape[0]
    low = which[1] == 0
    for half, block in ((which[0], act[...]), (1 - which[0], act_far[...])):
        at = pl.ds(half * size, size)
        left, right = block[:, :, :hidden], block[:, :, hidden:]
        keep[at] = left
        send[at] = right
        terms = times(flat(left), project[...]) + times(flat(right), project_far[...])
        terms = terms.reshape(size, 2 * rows, -1)
        first, second = terms[:, :rows], terms[:, rows:]
        stay[at] = jnp.where(low, first, second)
        leave[at] = jnp.where(low, second, first).astype(BF16)


def layer_kernel(stay, came, out):
    out[...] = (stay[...] + came[...].astype(F32)).astype(BF16)


def tok_kernel(grad, layer, expand, expand_far, out):
    hidden = expand.shape[1]
    chips, rows, features = layer.shape
    block = flat(grad[...])
    terms = times_turned(block[:, :hidden], expand[...]) + times_turned(block[:, hidden:], expand_far[...])
    parts = [layer[...].astype(F32), terms.reshape(chips, 2 * rows, features)]
    out[...] = jnp.concatenate(parts, axis=1).astype(BF16)


def pack_kernel(grad, act_send, keep, send):
    hidden = keep.shape[2]
    keep[...] = grad[:, :, :hidden]
    send[0] = act_send[...]
    send[1] = grad[:, :, hidden:]


def weight_grads_kernel(factor, panels, panels_far, act, grad, got, expand_grad, project_grad):
    own = panels.shape[1] // 2

    def sums(left, left_far, right, right_far):
        total = matmul(flat(left), flat(right), ((0,), (0,))) + matmul(flat(left_far), flat(right_far), ((0,), (0,)))
        return (total * factor).astype(BF16)

    project_grad[...] = sums(act[...], got[0], panels[:, own:], panels_far[:, own:])
    expand_grad[...] = sums(panels[:, :own], panels_far[:, :own], grad[...], got[1])


def final_kernel(sums, layer_out, token_grad):
    members, rows = sums.shape[0], layer_out.shape[0] // 2
    totals = []
    for first in (0, members // 2):
        total = sums[first].astype(F32)
        for at in range(first + 1, first + members // 2):
            total += sums[at].astype(F32)
        totals.append(total)
    layer_out[...] = jnp.concatenate([total[:rows] for total in totals], axis=0).astype(BF16)
    token_grad[...] = (totals[0][rows:] + totals[1][rows:]).astype(BF16)


def shards(tokens, expand, project, out_grad):
    rows, cols = lax.axis_size("row"), lax.axis_size("col")
    chips = cols // CORES
    own, features = tokens.shape
    hidden = expand.shape[1]
    wide, share, size = CORES * hidden, chips * own // rows, rows // PAIR
    over_col, along_z = col_groups(cols), row_groups(rows)
    factor = 1.0 / math.sqrt(own * cols)
    which = jnp.stack([lax.axis_index("row") // size, lax.axis_index("col") // (cols // PAIR)]).astype(jnp.int32)

    block = jnp.concatenate([tokens, out_grad], axis=0)
    copies = jnp.broadcast_to(block[None], (chips, *block.shape))
    project_far = swap_cores(after(project, copies))
    expand_far = swap_cores(after(expand, copies))
    panels = exchange(copies, "col", over_col)

    half_sums = array(size, share, wide)
    pre = call(
        pre_kernel,
        "pre",
        [array(rows, share, wide)],
        panels,
        expand,
        expand_far,
        ins=(0,),
        scratch=[pltpu.VMEM((chips, own, features), BF16), pltpu.SemaphoreType.DMA],
    )

    def back_terms(other, dtype, earlier):
        return call(
            functools.partial(back_kernel, other),
            "theirs" if other else "mine",
            [array(size, share, wide, dtype=dtype)],
            which,
            after(panels, earlier),
            project,
            project_far,
            ins=(1,),
            scratch=[pltpu.VMEM((size, own, features), BF16), pltpu.SemaphoreType.DMA],
        )

    theirs = back_terms(True, BF16, pre)
    came = swap_halves(theirs, "row")
    mine = back_terms(False, F32, theirs)
    pre = exchange(pre, "row", None)
    act, slope = call(
        act_kernel, "act", [array(share, wide), array(share, wide, dtype=F32)], pre
    )
    mixed = call(merge_kernel, "merge", [array(size, 2 * share, wide)], mine, came, act)
    mixed = exchange(mixed, "row", along_z)
    act, grad = call(grad_kernel, "grad", [half_sums, array(rows, share, wide)], mixed, slope)
    act_far = swap_halves(act, "row")
    grad = exchange(grad, "row", None)
    held = array(chips, own, hidden)
    stay, leave, act, act_send = call(
        out_kernel,
        "out",
        [array(chips, own // 2, features, dtype=F32), array(chips, own // 2, features), held, held],
        which,
        act,
        act_far,
        project,
        project_far,
    )
    layer_came = swap_halves(leave, "col")
    layer = call(layer_kernel, "layer", [array(chips, own // 2, features)], stay, layer_came)
    parts = call(
        tok_kernel, "tok", [array(chips, own + own // 2, features)], grad, layer, expand, expand_far
    )
    sums = exchange(parts, "col", over_col)
    grad, send = call(pack_kernel, "pack", [held, array(2, chips, own, hidden)], after(grad, parts), act_send)
    got = swap_cores(send)
    panels_far = swap_cores(after(panels, parts))
    expand_grad, project_grad = call(
        functools.partial(weight_grads_kernel, factor),
        "grads",
        [array(features, hidden), array(hidden, features)],
        panels,
        panels_far,
        act,
        grad,
        got,
    )
    shard = array(own, features)
    layer_out, token_grad = call(final_kernel, "final", [shard, shard], after(sums, expand_grad))
    return (layer_out, token_grad, expand_grad, project_grad)


def solution(mesh):
    placed = (P("col", "row"), P("row", "col"), P("col", "row"), P("col", "row"))
    return jax.shard_map(
        shards,
        mesh=mesh,
        in_specs=placed,
        out_specs=(P("col", "row"), P("col", "row"), P("row", "col"), P("col", "row")),
        check_vma=False,
    )
```

```python
import functools
import math

import jax
import jax.numpy as jnp
from jax import lax
from jax.experimental import pallas as pl
from jax.experimental.pallas import tpu as pltpu
from jax.sharding import PartitionSpec as P

SLOPE_C = math.sqrt(2.0 / math.pi)
CUBIC = 0.044715
CORES = 2
PAIR = 2
UNIT = 600_000_000
COSTS = dict(pre=(100, 10), theirs=(2.5, 1), mine=(2.5, 1), act=(0, 1), merge=(0, 1), grad=(0, 1), out=(100, 1), layer=(1, 1), tok=(0, 1), pack=(2.5, 1), grads=(2, 1), final=(0, 1))
F32, BF16 = jnp.float32, jnp.bfloat16
VMEM_BYTES = 12 << 20
MOST_VMEM_BYTES = 60 << 20
IN_VMEM = pl.BlockSpec(memory_space=pltpu.VMEM)
ANYWHERE = pl.BlockSpec(memory_space=pl.ANY)


def gelu_and_slope(value):
    inner = SLOPE_C * (value + CUBIC * value * value * value)
    tanh_value = jnp.tanh(inner)
    gelu = 0.5 * value * (1.0 + tanh_value)
    slope = 0.5 * (1.0 + tanh_value) + 0.5 * value * (1.0 - tanh_value * tanh_value) * SLOPE_C * (
        1.0 + 3.0 * CUBIC * value * value
    )
    return gelu, slope


def col_groups(cols):
    return [list(range(core, cols, CORES)) for core in range(CORES)]


def swap_cores(block):
    cols = lax.axis_size("col")
    return lax.ppermute(block, "col", [(at, at ^ 1) for at in range(cols)])


def row_groups(rows):
    step = rows // PAIR
    return [list(range(at * step, (at + 1) * step)) for at in range(PAIR)]


def swap_halves(block, axis):
    count = lax.axis_size(axis)
    return lax.ppermute(block, axis, [(at, (at + count // PAIR) % count) for at in range(count)])


def place():
    row, col = lax.axis_index("row"), lax.axis_index("col")
    rows, cols = lax.axis_size("row"), lax.axis_size("col")
    return lax.div(row, rows // PAIR), lax.div(col, cols // PAIR), lax.rem(col, CORES)


def exchange(parts, axis, groups):
    return lax.all_to_all(parts, axis, 0, 0, axis_index_groups=groups)


def after(block, earlier):
    return lax.optimization_barrier((block, earlier))[0]


def matmul(left, right, contract):
    return lax.dot_general(left, right, (contract, ((), ())), preferred_element_type=F32)


def times(left, right):
    return matmul(left, right, ((1,), (0,)))


def times_turned(left, right):
    return matmul(left, right, ((1,), (1,)))


def flat(block):
    return block.reshape(-1, block.shape[-1])


def array(*shape, dtype=BF16):
    return jax.ShapeDtypeStruct(shape, dtype)


def call(kernel, name, outs, *args, ins=(), scratch=(), limit=VMEM_BYTES):
    held = sum(math.prod(a.shape) * a.dtype.itemsize for a in (*args, *outs))
    one = len(outs) == 1
    products, touched = COSTS[name]
    return pl.pallas_call(
        kernel,
        out_shape=outs[0] if one else outs,
        in_specs=[ANYWHERE if at in ins else IN_VMEM for at in range(len(args))],
        out_specs=IN_VMEM if one else [IN_VMEM] * len(outs),
        scratch_shapes=scratch,
        compiler_params=pltpu.CompilerParams(vmem_limit_bytes=limit),
        cost_estimate=pl.CostEstimate(
            flops=int(products * UNIT), bytes_accessed=int(touched * held), transcendentals=0
        ),
    )(*args)


def pre_kernel(panels, expand, expand_far, out, held, sem):
    size, rows, hidden = out.shape[0] // PAIR, out.shape[1], out.shape[2]
    _, _, core = place()
    load = pltpu.make_async_copy(panels.at[:, pl.ds(0, held.shape[1])], held, sem)
    load.start()
    load.wait()
    for side, weight in ((core, expand), (1 - core, expand_far)):
        terms = times(flat(held[...]), weight[...]).astype(BF16)
        out[pl.ds(side * size, size)] = terms.reshape(size, rows, hidden)


def back_kernel(other, panels, project, project_far, out, held, weight, sem, weight_sem):
    own = held.shape[1]
    x_hi, _, core = place()
    near = (1 - x_hi if other else x_hi) == core
    load = pltpu.make_async_copy(panels.at[:, pl.ds(own, own)], held, sem)
    load.start()

    def bring(ref):
        copy = pltpu.make_async_copy(ref, weight, weight_sem)
        copy.start()
        copy.wait()

    pl.when(near)(lambda: bring(project))
    pl.when(jnp.logical_not(near))(lambda: bring(project_far))
    load.wait()
    out[...] = times_turned(flat(held[...]), weight[...]).astype(out.dtype).reshape(out.shape)


def added(ref, stop):
    total = ref[0, :stop].astype(F32)
    for at in range(1, ref.shape[0]):
        total += ref[at, :stop].astype(F32)
    return total


def act_kernel(sums, act, slope):
    gelu, slope[...] = gelu_and_slope(added(sums, sums.shape[1]))
    act[...] = gelu.astype(BF16)


def merge_kernel(mine, came, act, mixed):
    share = act.shape[0]
    mixed[:, :share] = (mine[...] + came[...].astype(F32)).astype(BF16)
    block = act[...]
    for at in range(mixed.shape[0]):
        mixed[at, share:] = block


def grad_kernel(mixed, slope, act, out):
    share = slope.shape[0]
    act[...] = mixed[:, share:]
    grad = (added(mixed, share) * slope[...]).astype(BF16)
    for at in range(out.shape[0]):
        out[at] = grad


def out_kernel(act, act_far, project, project_far, stay, leave, keep, send):
    chips, rows, features = stay.shape
    x_hi, x_lo, core = place()
    same, low = x_hi == core, x_lo == 0
    near, far = jnp.where(same, act[...], act_far[...]), jnp.where(same, act_far[...], act[...])
    keep[...] = near.reshape(keep.shape)
    send[...] = far.reshape(send.shape)
    terms = times(flat(near), project[...]) + times(flat(far), project_far[...])
    terms = terms.reshape(chips, 2 * rows, features)
    first, second = terms[:, :rows], terms[:, rows:]
    stay[...] = jnp.where(low, first, second)
    leave[...] = jnp.where(low, second, first).astype(BF16)


def layer_kernel(stay, came, out):
    out[...] = (stay[...] + came[...].astype(F32)).astype(BF16)


def two_cores(grad):
    size = grad.shape[0] // PAIR
    _, _, core = place()
    return [flat(grad[pl.ds(side * size, size)]) for side in (core, 1 - core)]


def tok_kernel(grad, layer, expand, expand_far, out):
    chips, rows, features = layer.shape
    near, far = two_cores(grad)
    terms = times_turned(near, expand[...]) + times_turned(far, expand_far[...])
    parts = [layer[...].astype(F32), terms.reshape(chips, 2 * rows, features)]
    out[...] = jnp.concatenate(parts, axis=1).astype(BF16)


def pack_kernel(grad, act_send, keep, send):
    near, far = two_cores(grad)
    keep[...] = near.reshape(keep.shape)
    send[0] = act_send[...]
    send[1] = far.reshape(keep.shape)


def weight_grads_kernel(factor, panels, panels_far, act, grad, got, expand_grad, project_grad):
    own = panels.shape[1] // 2

    def sums(left, left_far, right, right_far):
        total = matmul(flat(left), flat(right), ((0,), (0,))) + matmul(flat(left_far), flat(right_far), ((0,), (0,)))
        return (total * factor).astype(BF16)

    project_grad[...] = sums(act[...], got[0], panels[:, own:], panels_far[:, own:])
    expand_grad[...] = sums(panels[:, :own], panels_far[:, :own], grad[...], got[1])


def final_kernel(sums, layer_out, token_grad):
    members, rows = sums.shape[0], layer_out.shape[0] // 2
    totals = []
    for first in (0, members // 2):
        total = sums[first].astype(F32)
        for at in range(first + 1, first + members // 2):
            total += sums[at].astype(F32)
        totals.append(total)
    layer_out[...] = jnp.concatenate([total[:rows] for total in totals], axis=0).astype(BF16)
    token_grad[...] = (totals[0][rows:] + totals[1][rows:]).astype(BF16)


def shards(tokens, expand, project, out_grad):
    rows, cols = lax.axis_size("row"), lax.axis_size("col")
    chips = cols // CORES
    own, features = tokens.shape
    hidden = expand.shape[1]
    size = rows // PAIR
    share = chips * own // size
    over_col, along_z = col_groups(cols), row_groups(rows)
    factor = 1.0 / math.sqrt(own * cols)

    block = jnp.concatenate([tokens, out_grad], axis=0)
    copies = jnp.broadcast_to(block[None], (chips, *block.shape))
    project_far = swap_cores(after(project, copies))
    expand_far = swap_cores(after(expand, copies))
    panels = exchange(copies, "col", over_col)

    half_sums = array(size, share, hidden)
    pre = call(
        pre_kernel,
        "pre",
        [array(rows, share, hidden)],
        panels,
        expand,
        expand_far,
        ins=(0,),
        scratch=[pltpu.VMEM((chips, own, features), BF16), pltpu.SemaphoreType.DMA],
    )

    def back_terms(other, dtype, earlier):
        return call(
            functools.partial(back_kernel, other),
            "theirs" if other else "mine",
            [array(size, share, hidden, dtype=dtype)],
            after(panels, earlier),
            project,
            project_far,
            ins=(0, 1, 2),
            scratch=[
                pltpu.VMEM((chips, own, features), BF16),
                pltpu.VMEM(project.shape, BF16),
                pltpu.SemaphoreType.DMA,
                pltpu.SemaphoreType.DMA,
            ],
            limit=MOST_VMEM_BYTES,
        )

    theirs = back_terms(True, BF16, pre)
    came = swap_halves(theirs, "row")
    mine = back_terms(False, F32, theirs)
    pre = exchange(pre, "row", None)
    act, slope = call(act_kernel, "act", [array(share, hidden), array(share, hidden, dtype=F32)], pre)
    mixed = call(merge_kernel, "merge", [array(size, 2 * share, hidden)], mine, came, act)
    mixed = exchange(mixed, "row", along_z)
    act, grad = call(grad_kernel, "grad", [half_sums, array(rows, share, hidden)], mixed, slope)
    act_far = swap_halves(act, "row")
    grad = exchange(grad, "row", None)
    held = array(chips, own, hidden)
    stay, leave, act, act_send = call(
        out_kernel,
        "out",
        [array(chips, own // 2, features, dtype=F32), array(chips, own // 2, features), held, held],
        act,
        act_far,
        project,
        project_far,
    )
    layer_came = swap_halves(leave, "col")
    layer = call(layer_kernel, "layer", [array(chips, own // 2, features)], stay, layer_came)
    parts = call(
        tok_kernel, "tok", [array(chips, own + own // 2, features)], grad, layer, expand, expand_far
    )
    sums = exchange(parts, "col", over_col)
    grad, send = call(
        pack_kernel, "pack", [held, array(2, chips, own, hidden)], after(grad, parts), act_send
    )
    got = swap_cores(send)
    panels_far = swap_cores(after(panels, parts))
    expand_grad, project_grad = call(
        functools.partial(weight_grads_kernel, factor),
        "grads",
        [array(features, hidden), array(hidden, features)],
        panels,
        panels_far,
        act,
        grad,
        got,
    )
    shard = array(own, features)
    layer_out, token_grad = call(final_kernel, "final", [shard, shard], after(sums, expand_grad))
    return (layer_out, token_grad, expand_grad, project_grad)


def solution(mesh):
    placed = (P("col", "row"), P("row", "col"), P("col", "row"), P("col", "row"))
    return jax.shard_map(
        shards,
        mesh=mesh,
        in_specs=placed,
        out_specs=(P("col", "row"), P("col", "row"), P("row", "col"), P("col", "row")),
        check_vma=False,
    )
```

```python
import functools
import math

import jax
import jax.numpy as jnp
from jax import lax
from jax.experimental import pallas as pl
from jax.experimental.pallas import tpu as pltpu
from jax.sharding import PartitionSpec as P

SLOPE_C = math.sqrt(2.0 / math.pi)
CUBIC = 0.044715
CORES = 2
PAIR = 2
PIECES = 2
UNIT = 600_000_000
COSTS = dict(pre=(100, 10), theirs=(2.5, 1), mine=(2.5, 1), act=(0, 1), merge=(0, 1), grad=(0, 1), out=(100, 1), layer=(1, 1), tok=(0, 1), pack=(2.5, 1), grads=(2, 1), final=(0, 1))
F32, BF16 = jnp.float32, jnp.bfloat16
VMEM_BYTES = 12 << 20
MOST_VMEM_BYTES = 60 << 20
IN_VMEM = pl.BlockSpec(memory_space=pltpu.VMEM)
ANYWHERE = pl.BlockSpec(memory_space=pl.ANY)


def gelu_and_slope(value):
    inner = SLOPE_C * (value + CUBIC * value * value * value)
    tanh_value = jnp.tanh(inner)
    gelu = 0.5 * value * (1.0 + tanh_value)
    slope = 0.5 * (1.0 + tanh_value) + 0.5 * value * (1.0 - tanh_value * tanh_value) * SLOPE_C * (
        1.0 + 3.0 * CUBIC * value * value
    )
    return gelu, slope


def col_groups(cols):
    return [list(range(core, cols, CORES)) for core in range(CORES)]


def swap_cores(block):
    cols = lax.axis_size("col")
    return lax.ppermute(block, "col", [(at, at ^ 1) for at in range(cols)])


def row_groups(rows):
    step = rows // PAIR
    return [list(range(at * step, (at + 1) * step)) for at in range(PAIR)]


def swap_halves(block, axis):
    count = lax.axis_size(axis)
    return lax.ppermute(block, axis, [(at, (at + count // PAIR) % count) for at in range(count)])


def place():
    row, col = lax.axis_index("row"), lax.axis_index("col")
    rows, cols = lax.axis_size("row"), lax.axis_size("col")
    return lax.div(row, rows // PAIR), lax.div(col, cols // PAIR), lax.rem(col, CORES)


def exchange(parts, axis, groups):
    return lax.all_to_all(parts, axis, 0, 0, axis_index_groups=groups)


def after(block, earlier):
    return lax.optimization_barrier((block, earlier))[0]


def matmul(left, right, contract):
    return lax.dot_general(left, right, (contract, ((), ())), preferred_element_type=F32)


def times(left, right):
    return matmul(left, right, ((1,), (0,)))


def times_turned(left, right):
    return matmul(left, right, ((1,), (1,)))


def flat(block):
    return block.reshape(-1, block.shape[-1])


def array(*shape, dtype=BF16):
    return jax.ShapeDtypeStruct(shape, dtype)


def call(kernel, name, outs, *args, ins=(), scratch=(), limit=VMEM_BYTES):
    held = sum(math.prod(a.shape) * a.dtype.itemsize for a in (*args, *outs))
    one = len(outs) == 1
    products, touched = COSTS[name]
    return pl.pallas_call(
        kernel,
        out_shape=outs[0] if one else outs,
        in_specs=[ANYWHERE if at in ins else IN_VMEM for at in range(len(args))],
        out_specs=IN_VMEM if one else [IN_VMEM] * len(outs),
        scratch_shapes=scratch,
        compiler_params=pltpu.CompilerParams(vmem_limit_bytes=limit),
        cost_estimate=pl.CostEstimate(
            flops=int(products * UNIT), bytes_accessed=int(touched * held), transcendentals=0
        ),
    )(*args)


def pre_kernel(panels, expand, expand_far, out, held, sem):
    size, rows, hidden = out.shape[0] // PAIR, out.shape[1], out.shape[2]
    _, _, core = place()
    load = pltpu.make_async_copy(panels.at[:, pl.ds(0, held.shape[1])], held, sem)
    load.start()
    load.wait()
    for side, weight in ((core, expand), (1 - core, expand_far)):
        terms = times(flat(held[...]), weight[...]).astype(BF16)
        out[pl.ds(side * size, size)] = terms.reshape(size, rows, hidden)


def back_kernel(other, panels, project, project_far, out, held, weight, sem, weight_sems):
    own = held.shape[1]
    x_hi, _, core = place()
    near = (1 - x_hi if other else x_hi) == core
    load = pltpu.make_async_copy(panels.at[:, pl.ds(own, own)], held, sem)
    load.start()

    units = weight.shape[0] // PIECES
    rows = [pl.ds(at * units, units) for at in range(PIECES)]

    def bring(ref):
        for at in range(PIECES):
            pltpu.make_async_copy(ref.at[rows[at]], weight.at[rows[at]], weight_sems.at[at]).start()

    pl.when(near)(lambda: bring(project))
    pl.when(jnp.logical_not(near))(lambda: bring(project_far))
    load.wait()
    for at in range(PIECES):
        pltpu.make_async_copy(project.at[rows[at]], weight.at[rows[at]], weight_sems.at[at]).wait()
        terms = times_turned(flat(held[...]), weight[at * units : (at + 1) * units]).astype(out.dtype)
        out[:, :, at * units : (at + 1) * units] = terms.reshape(*out.shape[:2], units)


def added(ref, stop):
    total = ref[0, :stop].astype(F32)
    for at in range(1, ref.shape[0]):
        total += ref[at, :stop].astype(F32)
    return total


def act_kernel(sums, act, slope):
    gelu, slope[...] = gelu_and_slope(added(sums, sums.shape[1]))
    act[...] = gelu.astype(BF16)


def merge_kernel(mine, came, act, mixed):
    share = act.shape[0]
    mixed[:, :share] = (mine[...] + came[...].astype(F32)).astype(BF16)
    block = act[...]
    for at in range(mixed.shape[0]):
        mixed[at, share:] = block


def grad_kernel(mixed, slope, act, out):
    share = slope.shape[0]
    act[...] = mixed[:, share:]
    grad = (added(mixed, share) * slope[...]).astype(BF16)
    for at in range(out.shape[0]):
        out[at] = grad


def out_kernel(act, act_far, project, project_far, stay, leave, keep, send):
    chips, rows, features = stay.shape
    x_hi, x_lo, core = place()
    same, low = x_hi == core, x_lo == 0
    near, far = jnp.where(same, act[...], act_far[...]), jnp.where(same, act_far[...], act[...])
    keep[...] = near.reshape(keep.shape)
    send[...] = far.reshape(send.shape)
    terms = times(flat(near), project[...]) + times(flat(far), project_far[...])
    terms = terms.reshape(chips, 2 * rows, features)
    first, second = terms[:, :rows], terms[:, rows:]
    stay[...] = jnp.where(low, first, second)
    leave[...] = jnp.where(low, second, first).astype(BF16)


def layer_kernel(stay, came, out):
    out[...] = (stay[...] + came[...].astype(F32)).astype(BF16)


def two_cores(grad):
    size = grad.shape[0] // PAIR
    _, _, core = place()
    return [flat(grad[pl.ds(side * size, size)]) for side in (core, 1 - core)]


def tok_kernel(grad, layer, expand, expand_far, out):
    chips, rows, features = layer.shape
    near, far = two_cores(grad)
    terms = times_turned(near, expand[...]) + times_turned(far, expand_far[...])
    parts = [layer[...].astype(F32), terms.reshape(chips, 2 * rows, features)]
    out[...] = jnp.concatenate(parts, axis=1).astype(BF16)


def pack_kernel(grad, act_send, keep, send):
    near, far = two_cores(grad)
    keep[...] = near.reshape(keep.shape)
    send[0] = act_send[...]
    send[1] = far.reshape(keep.shape)


def weight_grads_kernel(factor, panels, panels_far, act, grad, got, expand_grad, project_grad):
    own = panels.shape[1] // 2

    def sums(left, left_far, right, right_far):
        total = matmul(flat(left), flat(right), ((0,), (0,))) + matmul(flat(left_far), flat(right_far), ((0,), (0,)))
        return (total * factor).astype(BF16)

    project_grad[...] = sums(act[...], got[0], panels[:, own:], panels_far[:, own:])
    expand_grad[...] = sums(panels[:, :own], panels_far[:, :own], grad[...], got[1])


def final_kernel(sums, layer_out, token_grad):
    members, rows = sums.shape[0], layer_out.shape[0] // 2
    totals = []
    for first in (0, members // 2):
        total = sums[first].astype(F32)
        for at in range(first + 1, first + members // 2):
            total += sums[at].astype(F32)
        totals.append(total)
    layer_out[...] = jnp.concatenate([total[:rows] for total in totals], axis=0).astype(BF16)
    token_grad[...] = (totals[0][rows:] + totals[1][rows:]).astype(BF16)


def shards(tokens, expand, project, out_grad):
    rows, cols = lax.axis_size("row"), lax.axis_size("col")
    chips = cols // CORES
    own, features = tokens.shape
    hidden = expand.shape[1]
    size = rows // PAIR
    share = chips * own // size
    over_col, along_z = col_groups(cols), row_groups(rows)
    factor = 1.0 / math.sqrt(own * cols)

    block = jnp.concatenate([tokens, out_grad], axis=0)
    copies = jnp.broadcast_to(block[None], (chips, *block.shape))
    project_far = swap_cores(after(project, copies))
    expand_far = swap_cores(after(expand, copies))
    panels = exchange(copies, "col", over_col)

    half_sums = array(size, share, hidden)
    pre = call(
        pre_kernel,
        "pre",
        [array(rows, share, hidden)],
        panels,
        expand,
        expand_far,
        ins=(0,),
        scratch=[pltpu.VMEM((chips, own, features), BF16), pltpu.SemaphoreType.DMA],
    )

    def back_terms(other, dtype, earlier):
        return call(
            functools.partial(back_kernel, other),
            "theirs" if other else "mine",
            [array(size, share, hidden, dtype=dtype)],
            after(panels, earlier),
            project,
            project_far,
            ins=(0, 1, 2),
            scratch=[
                pltpu.VMEM((chips, own, features), BF16),
                pltpu.VMEM(project.shape, BF16),
                pltpu.SemaphoreType.DMA,
                pltpu.SemaphoreType.DMA((PIECES,)),
            ],
            limit=MOST_VMEM_BYTES,
        )

    theirs = back_terms(True, BF16, pre)
    came = swap_halves(theirs, "row")
    mine = back_terms(False, F32, theirs)
    pre = exchange(pre, "row", None)
    act, slope = call(act_kernel, "act", [array(share, hidden), array(share, hidden, dtype=F32)], pre)
    mixed = call(merge_kernel, "merge", [array(size, 2 * share, hidden)], mine, came, act)
    mixed = exchange(mixed, "row", along_z)
    act, grad = call(grad_kernel, "grad", [half_sums, array(rows, share, hidden)], mixed, slope)
    act_far = swap_halves(act, "row")
    grad = exchange(grad, "row", None)
    held = array(chips, own, hidden)
    stay, leave, act, act_send = call(
        out_kernel,
        "out",
        [array(chips, own // 2, features, dtype=F32), array(chips, own // 2, features), held, held],
        act,
        act_far,
        project,
        project_far,
    )
    layer_came = swap_halves(leave, "col")
    layer = call(layer_kernel, "layer", [array(chips, own // 2, features)], stay, layer_came)
    parts = call(
        tok_kernel, "tok", [array(chips, own + own // 2, features)], grad, layer, expand, expand_far
    )
    sums = exchange(parts, "col", over_col)
    grad, send = call(
        pack_kernel, "pack", [held, array(2, chips, own, hidden)], after(grad, parts), act_send
    )
    got = swap_cores(send)
    panels_far = swap_cores(after(panels, parts))
    expand_grad, project_grad = call(
        functools.partial(weight_grads_kernel, factor),
        "grads",
        [array(features, hidden), array(hidden, features)],
        panels,
        panels_far,
        act,
        grad,
        got,
    )
    shard = array(own, features)
    layer_out, token_grad = call(final_kernel, "final", [shard, shard], after(sums, expand_grad))
    return (layer_out, token_grad, expand_grad, project_grad)


def solution(mesh):
    placed = (P("col", "row"), P("row", "col"), P("col", "row"), P("col", "row"))
    return jax.shard_map(
        shards,
        mesh=mesh,
        in_specs=placed,
        out_specs=(P("col", "row"), P("col", "row"), P("row", "col"), P("col", "row")),
        check_vma=False,
    )
```
